512 devices in a mesh: dp: 32 (over x, z_hi, core), seq: 16 (over y, z_lo).
Axes of the slice: x: 4, y: 4, z: 16 (z_hi: 4, z_lo: 4; z = z_hi * 4 + z_lo), core: 2. Of those that a mesh axis runs over, the one named last changes fastest.
Arguments:
- saved_acts: bfloat16 [196608, 3072], P(('dp', 'seq')), may hold values from -60 to 60
- out_grads: bfloat16 [196608, 1536], P(('dp', 'seq')), may hold values from -60 to 60
- master_weight: float32 [3072, 1536], P('seq', 'dp'), may hold values from -0.109375 to 0.109375
- first_moment: float32 [3072, 1536], P('seq', 'dp'), may hold values from -2 to 2
- second_moment: float32 [3072, 1536], P('seq', 'dp'), may hold values from 0.01 to 1
Outputs:
- new_master: float32 [3072, 1536], P('seq', 'dp')
- new_first: float32 [3072, 1536], P('seq', 'dp')
- new_second: float32 [3072, 1536], P('seq', 'dp')
- new_params: bfloat16 [3072, 1536], P('seq')
The draws below stay inside these ranges and needn't reach their ends.
All inputs are finite; a program needn't handle non-finite values.
Results may differ from the reference program's by a relative error of at most 0.0018.
Values may be sent and summed in bfloat16 or wider, within the bound.
No kernel may reach another device: no remote copies, remote signals or barrier semaphores. Data moves between devices by JAX's collectives and lax.ppermute only.
A program may use at most 64 MiB of HBM per device.

```python
import math
import jax
import jax.numpy as jnp
from jax import lax

D = 3072
FO = 1536
TOK_DEV = 384
TOKENS = 196608
N_DP = 32
N_SEQ = 16


def scaled_rows(key, row_total, col_total):
    key_rows, key_cols, key_base = jax.random.split(key, 3)
    row_scale = jnp.exp(jax.random.uniform(key_rows, (row_total, 1), jnp.float32) * math.log(10.0))
    ramp = jnp.arange(col_total, dtype=jnp.float32) / col_total
    jitter = jax.random.uniform(key_cols, (1, col_total), jnp.float32, -0.3, 0.3)
    col_scale = jnp.exp(ramp[None, :] * math.log(10.0) + jitter)
    base_vals = jnp.clip(jax.random.normal(key_base, (row_total, col_total), jnp.float32), -4.0, 4.0)
    return base_vals * row_scale * col_scale / 10.0


def draw_saved_acts(key, part):
    key = jax.random.fold_in(key, 11)
    return scaled_rows(key, TOKENS, D).astype(jnp.bfloat16)


def draw_out_grads(key, part):
    key = jax.random.fold_in(key, 12)
    return scaled_rows(key, TOKENS, FO).astype(jnp.bfloat16)


def shard_levels(stream_key, extent, pieces, smallest, largest):
    def one(dim, blocks):
        steps = jax.random.uniform(jax.random.fold_in(jax.random.fold_in(stream_key, 6), dim), (blocks,), jnp.float32, smallest / len(pieces), largest / len(pieces))
        return jnp.repeat(jnp.exp(steps), extent[dim] // blocks).reshape((-1,) + (1,) * (len(extent) - dim - 1))

    loudness = one(*pieces[0])
    for cut in pieces[1:]:
        loudness = loudness * one(*cut)
    return loudness


def noise(key, shape, scale, bound, pieces=(), kind=jnp.bfloat16):
    drawn = scale * jax.random.normal(key, shape, jnp.float32)
    if pieces:
        drawn = drawn * shard_levels(key, shape, pieces, -0.22, 0.18)
    return jnp.clip(drawn, -bound, bound).astype(kind)


def setup_inputs(seed: int = 0) -> dict:
    key_of = jax.random.split(jax.random.key(seed), 6)
    return {
        "saved_acts": draw_saved_acts(jax.random.fold_in(key_of[5], 71), 0),
        "out_grads": draw_out_grads(jax.random.fold_in(key_of[5], 71), 0),
        "master_weight": noise(key_of[2], (D, FO), D ** -0.5, 0.109375, ((0, 16), (1, 32)), jnp.float32),
        "first_moment": noise(key_of[3], (D, FO), 0.3, 2.0, ((0, 16), (1, 32)), jnp.float32),
        "second_moment": jnp.clip(jnp.exp(math.log(1.0) - 4.6051702 * jax.random.uniform(key_of[4], (D, FO), jnp.float32) ** shard_levels(key_of[4], (D, FO), ((0, 16), (1, 32)), -0.2, 0.2)), 0.01, 1.0),
    }


def add_slab(running, pair):
    term = jnp.dot(pair[0].T, pair[1], preferred_element_type=jnp.float32).astype(jnp.bfloat16)
    term = lax.optimization_barrier(term)
    return (running + term.astype(jnp.float32), None)

def reference(saved_acts, out_grads, master_weight, first_moment, second_moment):
    slab_total = N_DP * N_SEQ
    acts = saved_acts.reshape(slab_total, TOK_DEV, D)
    grads = out_grads.reshape(slab_total, TOK_DEV, FO)
    total, unused = lax.scan(add_slab, jnp.zeros((D, FO), jnp.float32), (acts, grads))
    rms = jnp.sqrt(jnp.sum(total * total) / (D * FO) + 1e-06)
    clip = jnp.minimum(1.0, 1.0 / rms)
    clipped = clip * total
    new_first = 0.9 * first_moment + 0.1 * clipped
    new_second = 0.95 * second_moment + 0.05 * clipped * clipped
    new_master = master_weight - 0.01 * (new_first / (jnp.sqrt(new_second) + 1e-08) + 0.1 * master_weight)
    return (new_master, new_first, new_second, new_master.astype(jnp.bfloat16))
```

```python
import jax
import jax.numpy as jnp
from jax import lax
from jax.experimental import pallas as pl
from jax.experimental.pallas import tpu as pltpu
from jax.sharding import Mesh, PartitionSpec as P

D = 3072
FO = 1536
TOK = 384
F32 = jnp.float32
F16 = jnp.float16
BF16 = jnp.bfloat16


def swap(value, axis):
    return lax.ppermute(value, axis, [(0, 1), (1, 0)])


def shift(value, axis, step):
    return lax.ppermute(value, axis, [(i, (i + step) % 4) for i in range(4)])


def trade(value, axes):
    return lax.all_to_all(value, axes, 0, 0, tiled=True)


def spread(scalar, axes, count):
    return trade(jnp.broadcast_to(scalar, (count, 8, 128)), axes)[:, 0, 0]


def pick(value, index):
    return lax.dynamic_index_in_dim(value, index, 0, keepdims=False)


def eighth(value):
    value = value * value
    value = value * value
    return value * value


def arrange_kernel(core_ref, grads_ref, acts_ref, mine_ref, other_ref):
    def write(even_ref, odd_ref):
        for x in range(4):
            block = grads_ref[:, x * 384:(x + 1) * 384].T
            for zh in range(4):
                to = (zh // 2) * 384 + x * 96 + (zh % 2) * 48
                even_ref[to:to + 48, :] = block[zh * 96:zh * 96 + 48]
                odd_ref[to:to + 48, :] = block[zh * 96 + 48:zh * 96 + 96]

    @pl.when(core_ref[0] == 0)
    def _():
        write(mine_ref, other_ref)

    @pl.when(core_ref[0] != 0)
    def _():
        write(other_ref, mine_ref)

    def peak(ref):
        top = jnp.abs(ref[0:16, :])
        for row in range(16, TOK, 16):
            top = jnp.maximum(top, jnp.abs(ref[row:row + 16, :]))
        return jnp.max(top.astype(F32))

    acts_peak, grads_peak = peak(acts_ref), peak(grads_ref)
    for ref in (mine_ref, other_ref):
        ref[768:784, 0:128] = jnp.full((16, 128), acts_peak, F32).astype(BF16)
        ref[768:784, 128:384] = jnp.full((16, 256), grads_peak, F32).astype(BF16)


def arrange(core, grads, acts):
    vmem = pl.BlockSpec(memory_space=pltpu.VMEM)
    return pl.pallas_call(
        arrange_kernel,
        out_shape=[jax.ShapeDtypeStruct((784, TOK), BF16)] * 2,
        in_specs=[pl.BlockSpec(memory_space=pltpu.SMEM), vmem, vmem],
        out_specs=[vmem, vmem],
        compiler_params=pltpu.CompilerParams(vmem_limit_bytes=24 << 20),
    )(core.reshape(1), grads, acts)


def own_kernel(cols_ref, acts_ref, out_ref):
    for half in range(2):
        rows = slice(384 * half, 384 * (half + 1))
        out_ref[rows, :] = jnp.dot(cols_ref[rows, :], acts_ref[...], preferred_element_type=F32).astype(BF16)


def own_terms(cols, acts):
    return pl.pallas_call(
        own_kernel,
        grid=(4,),
        out_shape=jax.ShapeDtypeStruct((768, D), BF16),
        in_specs=[pl.BlockSpec((784, TOK), lambda i: (0, 0)), pl.BlockSpec((TOK, 768), lambda i: (0, i))],
        out_specs=pl.BlockSpec((768, 768), lambda i: (0, i)),
        compiler_params=pltpu.CompilerParams(vmem_limit_bytes=32 << 20),
        cost_estimate=pl.CostEstimate(flops=2 * 768 * TOK * D, bytes_accessed=8 << 20, transcendentals=0),
    )(cols, acts)


def pair_kernel(mine_ref, their_ref, acts_ref, own_ref, over_x_ref, over_y_ref):
    step = pl.program_id(0)
    bound = jnp.zeros((16, 128), F32)
    for ref in (mine_ref, their_ref):
        bound = bound + TOK * ref[768:784, 0:128].astype(F32) * ref[768:784, 128:256].astype(F32)
    up = jnp.full((16, 128), 2.0 ** -14, F32)
    down = jnp.full((16, 128), 2.0 ** 14, F32)
    for k in range(-14, 14):
        over = bound > 2.0 ** (8 * k)
        up = jnp.where(over, up * 2.0, up)
        down = jnp.where(over, down * 0.5, down)
    scale = eighth(down[0:1, 0:1]) * 2.0 ** 15
    up = jnp.broadcast_to(up[0:1, 0:1], (8, 768))
    down = jnp.broadcast_to(down[0:1, 0:1], (8, 768))

    for half in range(2):
        rows = slice(384 * half, 384 * (half + 1))
        term = jnp.dot(their_ref[rows, :], acts_ref[...], preferred_element_type=F32).astype(BF16)
        total = (own_ref[rows, :].astype(F32) + term.astype(F32)) * scale
        if half == 0:
            for x in range(4):
                over_x_ref[x, pl.ds(pl.multiple_of(step * 96, 96), 96), :] = total[x * 96:(x + 1) * 96]
        else:
            over_y_ref[0, 0:384, :] = total
    over_y_ref[0, 384:392, :] = up
    over_y_ref[0, 392:400, :] = down

    @pl.when(step == 0)
    def _():
        for x in range(4):
            over_x_ref[x, 384:392, :] = up
            over_x_ref[x, 392:400, :] = down


def pair_sums(mine, theirs, acts, own):
    cols = pl.BlockSpec((784, TOK), lambda i: (0, 0))
    return pl.pallas_call(
        pair_kernel,
        grid=(4,),
        out_shape=[jax.ShapeDtypeStruct((4, 400, 768), F32)] * 2,
        in_specs=[cols, cols, pl.BlockSpec((TOK, 768), lambda i: (0, i)), pl.BlockSpec((768, 768), lambda i: (0, i))],
        out_specs=[pl.BlockSpec((4, 400, 768), lambda i: (0, 0, 0)), pl.BlockSpec((1, 400, 768), lambda i: (i, 0, 0))],
        compiler_params=pltpu.CompilerParams(vmem_limit_bytes=40 << 20),
        cost_estimate=pl.CostEstimate(flops=2 * 768 * TOK * D, bytes_accessed=18 << 20, transcendentals=0),
    )(mine, theirs, acts, own)


def add_parts(parts, rows, top):
    total, up, down = 0.0, None, None
    for part in parts:
        one_up = part[rows:rows + 1].astype(F32)
        one_down = part[rows + 8:rows + 9].astype(F32)
        total = total + part[:rows].astype(F32) * (eighth(one_up) * (1.0 / top))
        up = one_up if up is None else jnp.maximum(up, one_up)
        down = one_down if down is None else jnp.minimum(down, one_down)
    return total, up, down


def code(total, up, down, top):
    value = (total * (eighth(down) * top)).astype(F16).reshape(4, 96, 768)
    up = jnp.broadcast_to(up.astype(F16), (4, 8, 768))
    down = jnp.broadcast_to(down.astype(F16), (4, 8, 768))
    return jnp.concatenate([value, up, down], axis=1)


def local(acts, grads, master, first, second):
    core = lax.axis_index("c")
    x = lax.axis_index("x")
    y = lax.axis_index("y")

    their_acts = swap(acts, "c")
    mine, other = arrange(core, grads, acts)
    their_cols = swap(other, "c")
    own = own_terms(mine, acts)
    over_x, over_y = pair_sums(mine, their_cols, their_acts, own)
    from_x, from_y = [pick(over_x, x)], [pick(over_y, y)]
    for step in (2, 1, 3):
        from_x.append(shift(pick(over_x, (x + step) % 4).astype(F16), "x", step))
        from_y.append(shift(pick(over_y, (y + step) % 4).astype(F16), "y", step))

    send = code(*add_parts(from_x, 384, 2.0 ** 15), 2.0 ** 13)
    part = trade(send, "y")
    low = add_parts([part[i] for i in range(4)], 96, 2.0 ** 13)

    send = code(*add_parts(from_y, 384, 2.0 ** 15), 2.0 ** 13)
    parts = [pick(send, x)]
    for step in (2, 1, 3):
        parts.append(shift(pick(send, (x + step) % 4), "x", step))
    high = add_parts(parts, 96, 2.0 ** 13)

    tile = jnp.concatenate([low[0], high[0]], axis=0)
    up, down = jnp.maximum(low[1], high[1]), jnp.minimum(low[2], high[2])
    send = (tile * (eighth(down) * 2.0 ** 11)).astype(F16)
    send = send.reshape(4, 48, 4, 192).transpose(0, 2, 1, 3).reshape(16, 48, 192)
    up = jnp.broadcast_to(up[:, :64].astype(F16), (16, 48, 64))
    part = trade(jnp.concatenate([send, up], axis=2), ("zh", "zl"))
    up = part[:, :1, 192:193].astype(F32)
    grad = jnp.sum(part[:, :, :192].astype(F32) * (eighth(up) * 2.0 ** -11), axis=0)

    square = jnp.sum(grad * grad)
    square = square + swap(square, "c")
    square = jnp.sum(spread(square, ("x", "y"), 16))
    square = jnp.sum(spread(square, ("zh", "zl"), 16))
    rms = jnp.sqrt(square / (D * FO) + 1e-06)
    clip = jnp.minimum(1.0, 1.0 / rms)
    clipped = clip * grad.T
    new_first = 0.9 * first + 0.1 * clipped
    new_second = 0.95 * second + 0.05 * clipped * clipped
    new_master = master - 0.01 * (new_first / (jnp.sqrt(new_second) + 1e-08) + 0.1 * master)

    params = new_master.astype(BF16).T
    params = trade(jnp.broadcast_to(params, (4, 48, 192)), "zh")
    params = trade(jnp.broadcast_to(params, (4, 4, 48, 192)), "x").reshape(16, 48, 192)
    params = lax.all_gather(params, "c", axis=1, tiled=False)
    return (new_master, new_first, new_second, params.reshape(FO, 192).T)


def solution(mesh):
    fine = Mesh(mesh.devices.reshape(4, 4, 2, 4, 4), ("x", "zh", "c", "y", "zl"))
    dp, seq = ("x", "zh", "c"), ("y", "zl")
    return jax.shard_map(
        local,
        mesh=fine,
        in_specs=(P(dp + seq, None), P(dp + seq, None), P(seq, dp), P(seq, dp), P(seq, dp)),
        out_specs=(P(seq, dp), P(seq, dp), P(seq, dp), P(seq, None)),
        check_vma=False,
    )
```

```python
import jax
import jax.numpy as jnp
from jax import lax
from jax.experimental import pallas as pl
from jax.experimental.pallas import tpu as pltpu
from jax.sharding import Mesh, PartitionSpec as P

D = 3072
FO = 1536
TOK = 384
F32 = jnp.float32
F16 = jnp.float16
BF16 = jnp.bfloat16


def swap(value, axis):
    return lax.ppermute(value, axis, [(0, 1), (1, 0)])


def shift(value, axis, step):
    return lax.ppermute(value, axis, [(i, (i + step) % 4) for i in range(4)])


def trade(value, axes):
    return lax.all_to_all(value, axes, 0, 0, tiled=True)


def spread(scalar, axes, count):
    return trade(jnp.broadcast_to(scalar, (count, 8, 128)), axes)[:, 0, 0]


def pick(value, index):
    return lax.dynamic_index_in_dim(value, index, 0, keepdims=False)


def eighth(value):
    value = value * value
    value = value * value
    return value * value


def arrange_kernel(core_ref, grads_ref, acts_ref, mine_ref, other_ref):
    def write(even_ref, odd_ref):
        for x in range(4):
            block = grads_ref[:, x * 384:(x + 1) * 384].T
            for zh in range(4):
                to = x * 192 + zh * 48
                even_ref[to:to + 48, :] = block[zh * 96:zh * 96 + 48]
                odd_ref[to:to + 48, :] = block[zh * 96 + 48:zh * 96 + 96]

    @pl.when(core_ref[0] == 0)
    def _():
        write(mine_ref, other_ref)

    @pl.when(core_ref[0] != 0)
    def _():
        write(other_ref, mine_ref)

    def peak(ref):
        top = jnp.abs(ref[0:16, :])
        for row in range(16, TOK, 16):
            top = jnp.maximum(top, jnp.abs(ref[row:row + 16, :]))
        return jnp.max(top.astype(F32))

    acts_peak, grads_peak = peak(acts_ref), peak(grads_ref)
    for ref in (mine_ref, other_ref):
        ref[768:784, 0:128] = jnp.full((16, 128), acts_peak, F32).astype(BF16)
        ref[768:784, 128:384] = jnp.full((16, 256), grads_peak, F32).astype(BF16)


def arrange(core, grads, acts):
    vmem = pl.BlockSpec(memory_space=pltpu.VMEM)
    return pl.pallas_call(
        arrange_kernel,
        out_shape=[jax.ShapeDtypeStruct((784, TOK), BF16)] * 2,
        in_specs=[pl.BlockSpec(memory_space=pltpu.SMEM), vmem, vmem],
        out_specs=[vmem, vmem],
        compiler_params=pltpu.CompilerParams(vmem_limit_bytes=24 << 20),
    )(core.reshape(1), grads, acts)


def own_kernel(cols_ref, acts_ref, out_ref):
    for half in range(2):
        rows = slice(384 * half, 384 * (half + 1))
        out_ref[rows, :] = jnp.dot(cols_ref[rows, :], acts_ref[...], preferred_element_type=F32).astype(BF16)


def own_terms(cols, acts):
    return pl.pallas_call(
        own_kernel,
        grid=(4,),
        out_shape=jax.ShapeDtypeStruct((768, D), BF16),
        in_specs=[pl.BlockSpec((784, TOK), lambda i: (0, 0)), pl.BlockSpec((TOK, 768), lambda i: (0, i))],
        out_specs=pl.BlockSpec((768, 768), lambda i: (0, i)),
        compiler_params=pltpu.CompilerParams(vmem_limit_bytes=32 << 20),
        cost_estimate=pl.CostEstimate(flops=2 * 768 * TOK * D, bytes_accessed=8 << 20, transcendentals=0),
    )(cols, acts)


def pair_kernel(core_ref, mine_ref, their_ref, acts_ref, own_ref, out_ref):
    step = pl.program_id(0)
    core = core_ref[0]
    bound = jnp.zeros((16, 128), F32)
    for ref in (mine_ref, their_ref):
        bound = bound + TOK * ref[768:784, 0:128].astype(F32) * ref[768:784, 128:256].astype(F32)
    up = jnp.full((16, 128), 2.0 ** -14, F32)
    down = jnp.full((16, 128), 2.0 ** 14, F32)
    for k in range(-14, 14):
        over = bound > 2.0 ** (8 * k)
        up = jnp.where(over, up * 2.0, up)
        down = jnp.where(over, down * 0.5, down)
    scale = eighth(down[0:1, 0:1]) * 2.0 ** 15

    for half in range(2):
        rows = slice(384 * half, 384 * (half + 1))
        term = jnp.dot(their_ref[rows, :], acts_ref[...], preferred_element_type=F32).astype(BF16)
        total = (own_ref[rows, :].astype(F32) + term.astype(F32)) * scale
        for part in range(2):
            x = 2 * half + part
            u = jnp.where(core == 0, x, step)
            v = jnp.where(core == 0, step, x)
            out_ref[u, pl.ds(pl.multiple_of(v * 192, 192), 192), :] = total[part * 192:(part + 1) * 192]

    @pl.when(step == 0)
    def _():
        for u in range(4):
            out_ref[u, 768:776, :] = jnp.broadcast_to(up[0:1, 0:1], (8, 768))
            out_ref[u, 776:784, :] = jnp.broadcast_to(down[0:1, 0:1], (8, 768))


def pair_sums(core, mine, theirs, acts, own):
    cols = pl.BlockSpec((784, TOK), lambda i: (0, 0))
    return pl.pallas_call(
        pair_kernel,
        grid=(4,),
        out_shape=jax.ShapeDtypeStruct((4, 784, 768), F32),
        in_specs=[
            pl.BlockSpec(memory_space=pltpu.SMEM),
            cols,
            cols,
            pl.BlockSpec((TOK, 768), lambda i: (0, i)),
            pl.BlockSpec((768, 768), lambda i: (0, i)),
        ],
        out_specs=pl.BlockSpec((4, 784, 768), lambda i: (0, 0, 0)),
        compiler_params=pltpu.CompilerParams(vmem_limit_bytes=40 << 20),
        cost_estimate=pl.CostEstimate(flops=2 * 768 * TOK * D, bytes_accessed=18 << 20, transcendentals=0),
    )(core.reshape(1), mine, theirs, acts, own)


def add_parts(parts, rows, top):
    total, up, down = 0.0, None, None
    for part in parts:
        one_up = part[rows:rows + 1].astype(F32)
        one_down = part[rows + 8:rows + 9].astype(F32)
        total = total + part[:rows].astype(F32) * (eighth(one_up) * (1.0 / top))
        up = one_up if up is None else jnp.maximum(up, one_up)
        down = one_down if down is None else jnp.minimum(down, one_down)
    return total, up, down


def code(total, up, down, top):
    value = (total * (eighth(down) * top)).astype(F16).reshape(4, 192, 768)
    up = jnp.broadcast_to(up.astype(F16), (4, 8, 768))
    down = jnp.broadcast_to(down.astype(F16), (4, 8, 768))
    return jnp.concatenate([value, up, down], axis=1)


def z_kernel(tile_ref, up_ref, down_ref, out_ref):
    scale = eighth(down_ref[0:1, 0:1]) * 2.0 ** 11
    for zh in range(4):
        for zl in range(4):
            piece = tile_ref[zh * 48:(zh + 1) * 48, zl * 192:(zl + 1) * 192]
            out_ref[zh * 4 + zl, :, 0:192] = piece * scale
            out_ref[zh * 4 + zl, :, 192:256] = jnp.broadcast_to(up_ref[0:1, 0:1], (48, 64))


def z_pieces(tile, up, down):
    vmem = pl.BlockSpec(memory_space=pltpu.VMEM)
    return pl.pallas_call(
        z_kernel,
        out_shape=jax.ShapeDtypeStruct((16, 48, 256), F32),
        in_specs=[vmem, vmem, vmem],
        out_specs=vmem,
        compiler_params=pltpu.CompilerParams(vmem_limit_bytes=24 << 20),
    )(tile, up, down)


def cross_trade(value, first):
    groups = []
    for core in range(2):
        for a in range(4):
            fours = [(b, core, a) if core == first else (a, core, b) for b in range(4)]
            groups.append([(x * 2 + c) * 4 + y for x, c, y in fours])
    return lax.all_to_all(value, ("x", "c", "y"), 0, 0, axis_index_groups=groups, tiled=True)


def local(acts, grads, master, first, second):
    core = lax.axis_index("c")
    x = lax.axis_index("x")
    y = lax.axis_index("y")

    their_acts = swap(acts, "c")
    mine, other = arrange(core, grads, acts)
    their_cols = swap(other, "c")
    own = own_terms(mine, acts)
    part = cross_trade(pair_sums(core, mine, their_cols, their_acts, own).astype(F16), 0)
    send = code(*add_parts([part[i] for i in range(4)], 768, 2.0 ** 15), 2.0 ** 13)
    part = cross_trade(send, 1)
    tile, up, down = add_parts([part[i] for i in range(4)], 192, 2.0 ** 13)

    part = trade(z_pieces(tile, up, down).astype(F16), ("zh", "zl"))
    up = part[:, :1, 192:193].astype(F32)
    grad = jnp.sum(part[:, :, :192].astype(F32) * (eighth(up) * 2.0 ** -11), axis=0)

    square = jnp.sum(grad * grad)
    square = jnp.sum(spread(square, ("x", "y", "c"), 32))
    square = jnp.sum(spread(square, ("zh", "zl"), 16))
    rms = jnp.sqrt(square / (D * FO) + 1e-06)
    clip = jnp.minimum(1.0, 1.0 / rms)
    clipped = clip * grad.T
    new_first = 0.9 * first + 0.1 * clipped
    new_second = 0.95 * second + 0.05 * clipped * clipped
    new_master = master - 0.01 * (new_first / (jnp.sqrt(new_second) + 1e-08) + 0.1 * master)

    params = new_master.astype(BF16).T
    params = trade(jnp.broadcast_to(params, (4, 48, 192)), "zh")
    params = trade(jnp.broadcast_to(params, (4, 4, 48, 192)), "x").reshape(16, 48, 192)
    theirs = swap(params, "c")
    params = jnp.where(core == 0, jnp.stack([params, theirs], 1), jnp.stack([theirs, params], 1))
    return (new_master, new_first, new_second, params.reshape(FO, 192).T)


def solution(mesh):
    fine = Mesh(mesh.devices.reshape(4, 4, 2, 4, 4), ("x", "zh", "c", "y", "zl"))
    dp, seq = ("x", "zh", "c"), ("y", "zl")
    return jax.shard_map(
        local,
        mesh=fine,
        in_specs=(P(dp + seq, None), P(dp + seq, None), P(seq, dp), P(seq, dp), P(seq, dp)),
        out_specs=(P(seq, dp), P(seq, dp), P(seq, dp), P(seq, None)),
        check_vma=False,
    )
```

```python
import functools

import jax
import jax.numpy as jnp
from jax import lax
from jax.experimental import pallas as pl
from jax.experimental.pallas import tpu as pltpu
from jax.sharding import Mesh, PartitionSpec as P

D = 3072
FO = 1536
TOK = 384
F32 = jnp.float32
F16 = jnp.float16
BF16 = jnp.bfloat16


def swap(value, axis):
    return lax.ppermute(value, axis, [(0, 1), (1, 0)])


def trade(value, axes):
    return lax.all_to_all(value, axes, 0, 0, tiled=True)


def eighth(value):
    value = value * value
    value = value * value
    return value * value


def arrange_kernel(core_ref, grads_ref, acts_ref, mine_ref, other_ref):
    def write(even_ref, odd_ref):
        for x in range(4):
            block = grads_ref[:, x * 384:(x + 1) * 384].T
            for zh in range(4):
                to = (zh // 2) * 384 + x * 96 + (zh % 2) * 48
                even_ref[to:to + 48, :] = block[zh * 96:zh * 96 + 48]
                odd_ref[to:to + 48, :] = block[zh * 96 + 48:zh * 96 + 96]

    @pl.when(core_ref[0] == 0)
    def _():
        write(mine_ref, other_ref)

    @pl.when(core_ref[0] != 0)
    def _():
        write(other_ref, mine_ref)

    def peak(ref):
        top = jnp.abs(ref[0:16, :])
        for row in range(16, TOK, 16):
            top = jnp.maximum(top, jnp.abs(ref[row:row + 16, :]))
        return jnp.max(top.astype(F32))

    acts_peak, grads_peak = peak(acts_ref), peak(grads_ref)
    for ref in (mine_ref, other_ref):
        ref[768:784, 0:128] = jnp.full((16, 128), acts_peak, F32).astype(BF16)
        ref[768:784, 128:384] = jnp.full((16, 256), grads_peak, F32).astype(BF16)


def arrange(core, grads, acts):
    vmem = pl.BlockSpec(memory_space=pltpu.VMEM)
    return pl.pallas_call(
        arrange_kernel,
        out_shape=[jax.ShapeDtypeStruct((784, TOK), BF16)] * 2,
        in_specs=[pl.BlockSpec(memory_space=pltpu.SMEM), vmem, vmem],
        out_specs=[vmem, vmem],
        compiler_params=pltpu.CompilerParams(vmem_limit_bytes=24 << 20),
    )(core.reshape(1), grads, acts)


def own_kernel(cols_ref, acts_ref, out_ref):
    for half in range(2):
        rows = slice(384 * half, 384 * (half + 1))
        out_ref[rows, :] = jnp.dot(cols_ref[rows, :], acts_ref[...], preferred_element_type=F32).astype(BF16)


def own_terms(cols, acts):
    return pl.pallas_call(
        own_kernel,
        grid=(4,),
        out_shape=jax.ShapeDtypeStruct((768, D), BF16),
        in_specs=[pl.BlockSpec((784, TOK), lambda i: (0, 0)), pl.BlockSpec((TOK, 768), lambda i: (0, i))],
        out_specs=pl.BlockSpec((768, 768), lambda i: (0, i)),
        compiler_params=pltpu.CompilerParams(vmem_limit_bytes=32 << 20),
        cost_estimate=pl.CostEstimate(flops=2 * 768 * TOK * D, bytes_accessed=8 << 20, transcendentals=0),
    )(cols, acts)


def pair_kernel(core_ref, mine_ref, their_ref, acts_ref, own_ref, out_ref, *, half):
    step = pl.program_id(0)
    core = core_ref[0]
    bound = jnp.zeros((16, 128), F32)
    for ref in (mine_ref, their_ref):
        bound = bound + TOK * ref[768:784, 0:128].astype(F32) * ref[768:784, 128:256].astype(F32)
    up = jnp.full((16, 128), 2.0 ** -14, F32)
    down = jnp.full((16, 128), 2.0 ** 14, F32)
    for k in range(-14, 14):
        over = bound > 2.0 ** (8 * k)
        up = jnp.where(over, up * 2.0, up)
        down = jnp.where(over, down * 0.5, down)
    scale = eighth(down[0:1, 0:1]) * 2.0 ** 15

    rows = slice(384 * half, 384 * (half + 1))
    term = jnp.dot(their_ref[rows, :], acts_ref[...], preferred_element_type=F32).astype(BF16)
    total = (own_ref[...].astype(F32) + term.astype(F32)) * scale
    for x in range(4):
        u = jnp.where(core == 0, x, step)
        v = jnp.where(core == 0, step, x)
        out_ref[u, pl.ds(pl.multiple_of(v * 96, 96), 96), :] = total[x * 96:(x + 1) * 96]

    if half == 1:
        @pl.when(step == 0)
        def _():
            for u in range(4):
                out_ref[u, 384:392, :] = jnp.broadcast_to(up[0:1, 0:1], (8, 768))
                out_ref[u, 392:400, :] = jnp.broadcast_to(down[0:1, 0:1], (8, 768))


def pair_sums(half, core, mine, theirs, acts, own):
    cols = pl.BlockSpec((784, TOK), lambda i: (0, 0))
    rows = 400 if half else 384
    return pl.pallas_call(
        functools.partial(pair_kernel, half=half),
        grid=(4,),
        out_shape=jax.ShapeDtypeStruct((4, rows, 768), F32),
        in_specs=[
            pl.BlockSpec(memory_space=pltpu.SMEM),
            cols,
            cols,
            pl.BlockSpec((TOK, 768), lambda i: (0, i)),
            pl.BlockSpec((384, 768), lambda i: (half, i)),
        ],
        out_specs=pl.BlockSpec((4, rows, 768), lambda i: (0, 0, 0)),
        compiler_params=pltpu.CompilerParams(vmem_limit_bytes=32 << 20),
        cost_estimate=pl.CostEstimate(flops=768 * TOK * D, bytes_accessed=9 << 20, transcendentals=0),
    )(core.reshape(1), mine, theirs, acts, own)


def scales(parts, rows):
    ups = [part[rows:rows + 1].astype(F32) for part in parts]
    downs = [part[rows + 8:rows + 9].astype(F32) for part in parts]
    return [eighth(up) for up in ups], functools.reduce(jnp.maximum, ups), functools.reduce(jnp.minimum, downs)


def add_parts(parts, factors, rows, top):
    return sum(part[:rows].astype(F32) * (factor * (1.0 / top)) for part, factor in zip(parts, factors))


def pack(ref, value):
    ref[0:48, :] = value[:, 0:128]
    ref[48:72, 0:64] = value[0:24, 128:192]
    ref[48:72, 64:128] = value[24:48, 128:192]


def unpack(ref, at, value):
    ref[at:at + 48, 0:128] = value[0:48]
    ref[at:at + 24, 128:192] = value[48:72, 0:64]
    ref[at + 24:at + 48, 128:192] = value[48:72, 64:128]


def z_kernel(tile_ref, up_ref, down_ref, out_ref):
    scale = eighth(down_ref[0:1, 0:1]) * 2.0 ** 11
    for zh in range(4):
        for zl in range(4):
            piece = tile_ref[zh * 48:(zh + 1) * 48, zl * 192:(zl + 1) * 192]
            pack(out_ref.at[zh * 4 + zl], piece * scale)
            out_ref[zh * 4 + zl, 72:80, :] = jnp.broadcast_to(up_ref[0:1, 0:1], (8, 128))


def z_pieces(tile, up, down):
    vmem = pl.BlockSpec(memory_space=pltpu.VMEM)
    return pl.pallas_call(
        z_kernel,
        out_shape=jax.ShapeDtypeStruct((16, 80, 128), F32),
        in_specs=[vmem, vmem, vmem],
        out_specs=vmem,
        compiler_params=pltpu.CompilerParams(vmem_limit_bytes=24 << 20),
    )(tile, up, down)


def square_kernel(grad_ref, out_ref):
    grad = grad_ref[...]
    out_ref[...] = jnp.full(out_ref.shape, jnp.sum(grad * grad), F32)


def sum_kernel(part_ref, out_ref):
    total = part_ref[0]
    for i in range(1, part_ref.shape[0]):
        total = total + part_ref[i]
    for i in range(out_ref.shape[0]):
        out_ref[i] = total


def to_send(kernel, count, value):
    vmem = pl.BlockSpec(memory_space=pltpu.VMEM)
    return pl.pallas_call(
        kernel, out_shape=jax.ShapeDtypeStruct((count, 1, 128), F32), in_specs=[vmem], out_specs=vmem
    )(value)


def update_kernel(square_ref, grad_ref, master_ref, first_ref, second_ref, *refs):
    new_master_ref, new_first_ref, new_second_ref, params_ref, tile_ref = refs
    square = square_ref[0]
    for i in range(1, 16):
        square = square + square_ref[i]
    rms = jnp.sqrt(square[:, 0:1] / (D * FO) + 1e-06)
    clip = jnp.minimum(1.0, 1.0 / rms)
    unpack(tile_ref, 0, grad_ref[...])
    clipped = clip * tile_ref[...]
    master = master_ref[...]
    new_first = 0.9 * first_ref[...] + 0.1 * clipped
    new_second = 0.95 * second_ref[...] + 0.05 * clipped * clipped
    new_master = master - 0.01 * (new_first / (jnp.sqrt(new_second) + 1e-08) + 0.1 * master)
    new_master_ref[...], new_first_ref[...], new_second_ref[...] = new_master, new_first, new_second
    for i in range(4):
        params_ref[i] = new_master.astype(BF16)


def update(square, grad, *state):
    vmem = pl.BlockSpec(memory_space=pltpu.VMEM)
    tile = jax.ShapeDtypeStruct((48, 192), F32)
    return pl.pallas_call(
        update_kernel,
        out_shape=[tile, tile, tile, jax.ShapeDtypeStruct((4, 48, 192), BF16)],
        in_specs=[vmem] * 5,
        out_specs=[vmem] * 4,
        scratch_shapes=[pltpu.VMEM((48, 192), F32)],
    )(square, grad, *state)


def cross_trade(value, first):
    groups = []
    for core in range(2):
        for a in range(4):
            fours = [(b, core, a) if core == first else (a, core, b) for b in range(4)]
            groups.append([(x * 2 + c) * 4 + y for x, c, y in fours])
    return lax.all_to_all(value, ("x", "c", "y"), 0, 0, axis_index_groups=groups, tiled=True)


def local(acts, grads, master, first, second):
    core = lax.axis_index("c")

    their_acts = swap(acts, "c")
    mine, other = arrange(core, grads, acts)
    their_cols = swap(other, "c")
    own = own_terms(mine, acts)
    halves = [pair_sums(half, core, mine, their_cols, their_acts, own) for half in range(2)]
    part = cross_trade(jnp.concatenate(halves, axis=1).astype(F16), 0)
    parts = [part[i] for i in range(4)]
    factors, up, down = scales(parts, 768)
    total = add_parts(parts, factors, 768, 2.0 ** 15) * (eighth(down) * 2.0 ** 13)
    send = [total[:384].reshape(4, 96, 768), total[384:].reshape(4, 96, 768)]
    send += [jnp.broadcast_to(row, (4, 8, 768)) for row in (up, down)]
    part = cross_trade(jnp.concatenate([part.astype(F16) for part in send], axis=1), 1)
    parts = [part[i] for i in range(4)]
    factors, up, down = scales(parts, 192)
    tile = add_parts(parts, factors, 192, 2.0 ** 13)

    part = trade(z_pieces(tile, up, down).astype(F16), ("zh", "zl"))
    ups = part[:, 72:73, 0:1].astype(F32)
    grad = jnp.sum(part[:, :72].astype(F32) * (eighth(ups) * 2.0 ** -11), axis=0)

    square = trade(to_send(square_kernel, 32, grad), ("x", "y", "c"))
    square = trade(to_send(sum_kernel, 16, square), ("zh", "zl"))
    *outs, params = update(square, grad, master.T, first.T, second.T)
    params = trade(params, "zh")
    params = trade(jnp.broadcast_to(params, (4, 4, 48, 192)), "x").reshape(16, 48, 192)
    theirs = swap(params, "c")
    params = jnp.where(core == 0, jnp.stack([params, theirs], 1), jnp.stack([theirs, params], 1))
    return (*[out.T for out in outs], params.reshape(FO, 192).T)


def solution(mesh):
    fine = Mesh(mesh.devices.reshape(4, 4, 2, 4, 4), ("x", "zh", "c", "y", "zl"))
    dp, seq = ("x", "zh", "c"), ("y", "zl")
    return jax.shard_map(
        local,
        mesh=fine,
        in_specs=(P(dp + seq, None), P(dp + seq, None), P(seq, dp), P(seq, dp), P(seq, dp)),
        out_specs=(P(seq, dp), P(seq, dp), P(seq, dp), P(seq, None)),
        check_vma=False,
    )
```

```python
import functools

import jax
import jax.numpy as jnp
from jax import lax
from jax.experimental import pallas as pl
from jax.experimental.pallas import tpu as pltpu
from jax.sharding import Mesh, PartitionSpec as P

D = 3072
FO = 1536
TOK = 384
F32 = jnp.float32
F16 = jnp.float16
BF16 = jnp.bfloat16


def swap(value, axis):
    return lax.ppermute(value, axis, [(0, 1), (1, 0)])


def trade(value, axes):
    return lax.all_to_all(value, axes, 0, 0, tiled=True)


def eighth(value):
    value = value * value
    value = value * value
    return value * value


def peak(ref):
    top = jnp.abs(ref[0:16, :])
    for row in range(16, TOK, 16):
        top = jnp.maximum(top, jnp.abs(ref[row:row + 16, :]))
    return jnp.max(top.astype(F32))


def arrange_kernel(core_ref, grads_ref, mine_ref, other_ref):
    def write(even_ref, odd_ref):
        for x in range(4):
            block = grads_ref[:, x * 384:(x + 1) * 384].T
            for zh in range(4):
                to = (zh // 2) * 384 + x * 96 + (zh % 2) * 48
                even_ref[to:to + 48, :] = block[zh * 96:zh * 96 + 48]
                odd_ref[to:to + 48, :] = block[zh * 96 + 48:zh * 96 + 96]

    @pl.when(core_ref[0] == 0)
    def _():
        write(mine_ref, other_ref)

    @pl.when(core_ref[0] != 0)
    def _():
        write(other_ref, mine_ref)

    top = jnp.full((16, TOK), peak(grads_ref), F32).astype(BF16)
    mine_ref[768:784, :] = top
    other_ref[768:784, :] = top


def arrange(core, grads):
    vmem = pl.BlockSpec(memory_space=pltpu.VMEM)
    return pl.pallas_call(
        arrange_kernel,
        out_shape=[jax.ShapeDtypeStruct((784, TOK), BF16)] * 2,
        in_specs=[pl.BlockSpec(memory_space=pltpu.SMEM), vmem],
        out_specs=[vmem, vmem],
        compiler_params=pltpu.CompilerParams(vmem_limit_bytes=8 << 20),
    )(core.reshape(1), grads)


def own_kernel(cols_ref, acts_ref, out_ref, peak_ref):
    peak_ref[...] = jnp.full((8, 128), peak(acts_ref), F32)
    for y in range(4):
        lanes = slice(768 * y, 768 * (y + 1))
        for half in range(2):
            rows = slice(384 * half, 384 * (half + 1))
            term = jnp.dot(cols_ref[rows, :], acts_ref[:, lanes], preferred_element_type=F32)
            out_ref[rows, lanes] = term.astype(BF16)


def own_terms(cols, acts):
    vmem = pl.BlockSpec(memory_space=pltpu.VMEM)
    return pl.pallas_call(
        own_kernel,
        out_shape=[jax.ShapeDtypeStruct((768, D), BF16), jax.ShapeDtypeStruct((8, 128), F32)],
        in_specs=[vmem, vmem],
        out_specs=[vmem, vmem],
        compiler_params=pltpu.CompilerParams(vmem_limit_bytes=14 << 20),
        cost_estimate=pl.CostEstimate(flops=2 * 768 * TOK * D, bytes_accessed=8 << 20, transcendentals=0),
    )(cols, acts)


def pair_kernel(core_ref, mine_ref, their_ref, acts_ref, own_ref, peak_ref, out_ref):
    core = core_ref[0]
    bound = peak_ref[...] * mine_ref[768:784, 0:128].astype(F32)[0:8]
    bound = TOK * (bound + peak(acts_ref) * their_ref[768:784, 0:128].astype(F32)[0:8])
    up = jnp.full((8, 128), 2.0 ** -14, F32)
    down = jnp.full((8, 128), 2.0 ** 14, F32)
    for k in range(-14, 14):
        over = bound > 2.0 ** (8 * k)
        up = jnp.where(over, up * 2.0, up)
        down = jnp.where(over, down * 0.5, down)
    scale = eighth(down[0:1, 0:1]) * 2.0 ** 15

    for half in range(2):
        rows = slice(384 * half, 384 * (half + 1))
        for y in range(4):
            lanes = slice(768 * y, 768 * (y + 1))
            term = jnp.dot(their_ref[rows, :], acts_ref[:, lanes], preferred_element_type=F32).astype(BF16)
            total = (own_ref[rows, lanes].astype(F32) + term.astype(F32)) * scale
            for x in range(4):
                u = jnp.where(core == 0, x, y)
                v = jnp.where(core == 0, y, x)
                at = pl.multiple_of(half * 384 + v * 96, 96)
                out_ref[u, pl.ds(at, 96), :] = total[x * 96:(x + 1) * 96]

    for u in range(4):
        out_ref[u, 768:776, :] = jnp.broadcast_to(up[0:1, 0:1], (8, 768))
        out_ref[u, 776:784, :] = jnp.broadcast_to(down[0:1, 0:1], (8, 768))


def pair_sums(core, mine, theirs, acts, own, own_peak):
    vmem = pl.BlockSpec(memory_space=pltpu.VMEM)
    return pl.pallas_call(
        pair_kernel,
        out_shape=jax.ShapeDtypeStruct((4, 784, 768), F32),
        in_specs=[pl.BlockSpec(memory_space=pltpu.SMEM)] + [vmem] * 5,
        out_specs=vmem,
        compiler_params=pltpu.CompilerParams(vmem_limit_bytes=24 << 20),
        cost_estimate=pl.CostEstimate(flops=2 * 768 * TOK * D, bytes_accessed=18 << 20, transcendentals=0),
    )(core.reshape(1), mine, theirs, acts, own, own_peak)


def scales(parts, rows):
    ups = [part[rows:rows + 1].astype(F32) for part in parts]
    downs = [part[rows + 8:rows + 9].astype(F32) for part in parts]
    return [eighth(up) for up in ups], functools.reduce(jnp.maximum, ups), functools.reduce(jnp.minimum, downs)


def add_parts(parts, factors, rows, top):
    return sum(part[:rows].astype(F32) * (factor * (1.0 / top)) for part, factor in zip(parts, factors))


def pack(ref, value):
    ref[0:48, :] = value[:, 0:128]
    ref[48:72, 0:64] = value[0:24, 128:192]
    ref[48:72, 64:128] = value[24:48, 128:192]


def unpack(ref, at, value):
    ref[at:at + 48, 0:128] = value[0:48]
    ref[at:at + 24, 128:192] = value[48:72, 0:64]
    ref[at + 24:at + 48, 128:192] = value[48:72, 64:128]


def z_kernel(tile_ref, up_ref, down_ref, out_ref):
    scale = eighth(down_ref[0:1, 0:1]) * 2.0 ** 11
    for zh in range(4):
        for zl in range(4):
            piece = tile_ref[zh * 48:(zh + 1) * 48, zl * 192:(zl + 1) * 192]
            pack(out_ref.at[zh * 4 + zl], piece * scale)
            out_ref[zh * 4 + zl, 72:80, :] = jnp.broadcast_to(up_ref[0:1, 0:1], (8, 128))


def z_pieces(tile, up, down):
    vmem = pl.BlockSpec(memory_space=pltpu.VMEM)
    return pl.pallas_call(
        z_kernel,
        out_shape=jax.ShapeDtypeStruct((16, 80, 128), F32),
        in_specs=[vmem, vmem, vmem],
        out_specs=vmem,
        compiler_params=pltpu.CompilerParams(vmem_limit_bytes=8 << 20),
    )(tile, up, down)


def square_kernel(grad_ref, out_ref):
    grad = grad_ref[...]
    out_ref[...] = jnp.full(out_ref.shape, jnp.sum(grad * grad), F32)


def sum_kernel(part_ref, out_ref):
    total = part_ref[0]
    for i in range(1, part_ref.shape[0]):
        total = total + part_ref[i]
    for i in range(out_ref.shape[0]):
        out_ref[i] = total


def to_send(kernel, count, value):
    vmem = pl.BlockSpec(memory_space=pltpu.VMEM)
    return pl.pallas_call(
        kernel, out_shape=jax.ShapeDtypeStruct((count, 1, 128), F32), in_specs=[vmem], out_specs=vmem
    )(value)


def update_kernel(square_ref, grad_ref, master_ref, first_ref, second_ref, *refs):
    new_master_ref, new_first_ref, new_second_ref, params_ref, tile_ref = refs
    square = square_ref[0]
    for i in range(1, 16):
        square = square + square_ref[i]
    rms = jnp.sqrt(square[:, 0:1] / (D * FO) + 1e-06)
    clip = jnp.minimum(1.0, 1.0 / rms)
    unpack(tile_ref, 0, grad_ref[...])
    clipped = clip * tile_ref[...]
    master = master_ref[...]
    new_first = 0.9 * first_ref[...] + 0.1 * clipped
    new_second = 0.95 * second_ref[...] + 0.05 * clipped * clipped
    new_master = master - 0.01 * (new_first / (jnp.sqrt(new_second) + 1e-08) + 0.1 * master)
    new_master_ref[...], new_first_ref[...], new_second_ref[...] = new_master, new_first, new_second
    for i in range(4):
        params_ref[i] = new_master.astype(BF16)


def update(square, grad, *state):
    vmem = pl.BlockSpec(memory_space=pltpu.VMEM)
    tile = jax.ShapeDtypeStruct((48, 192), F32)
    return pl.pallas_call(
        update_kernel,
        out_shape=[tile, tile, tile, jax.ShapeDtypeStruct((4, 48, 192), BF16)],
        in_specs=[vmem] * 5,
        out_specs=[vmem] * 4,
        scratch_shapes=[pltpu.VMEM((48, 192), F32)],
    )(square, grad, *state)


def cross_trade(value, first):
    groups = []
    for core in range(2):
        for a in range(4):
            fours = [(b, core, a) if core == first else (a, core, b) for b in range(4)]
            groups.append([(x * 2 + c) * 4 + y for x, c, y in fours])
    return lax.all_to_all(value, ("x", "c", "y"), 0, 0, axis_index_groups=groups, tiled=True)


def local(acts, grads, master, first, second):
    core = lax.axis_index("c")

    their_acts = swap(acts, "c")
    mine, other = arrange(core, grads)
    their_cols = swap(other, "c")
    own, own_peak = own_terms(mine, acts)
    sums = pair_sums(core, mine, their_cols, their_acts, own, own_peak)
    part = cross_trade(sums.astype(F16), 0)
    parts = [part[i] for i in range(4)]
    factors, up, down = scales(parts, 768)
    total = add_parts(parts, factors, 768, 2.0 ** 15) * (eighth(down) * 2.0 ** 13)
    send = [total[:384].reshape(4, 96, 768), total[384:].reshape(4, 96, 768)]
    send += [jnp.broadcast_to(row, (4, 8, 768)) for row in (up, down)]
    part = cross_trade(jnp.concatenate([part.astype(F16) for part in send], axis=1), 1)
    parts = [part[i] for i in range(4)]
    factors, up, down = scales(parts, 192)
    tile = add_parts(parts, factors, 192, 2.0 ** 13)

    part = trade(z_pieces(tile, up, down).astype(F16), ("zh", "zl"))
    ups = part[:, 72:73, 0:1].astype(F32)
    grad = jnp.sum(part[:, :72].astype(F32) * (eighth(ups) * 2.0 ** -11), axis=0)

    square = trade(to_send(square_kernel, 32, grad), ("x", "y", "c"))
    square = trade(to_send(sum_kernel, 16, square), ("zh", "zl"))
    *outs, params = update(square, grad, master.T, first.T, second.T)
    params = trade(params, "zh")
    params = trade(jnp.broadcast_to(params, (4, 4, 48, 192)), "x").reshape(16, 48, 192)
    theirs = swap(params, "c")
    params = jnp.where(core == 0, jnp.stack([params, theirs], 1), jnp.stack([theirs, params], 1))
    return (*[out.T for out in outs], params.reshape(FO, 192).T)


def solution(mesh):
    fine = Mesh(mesh.devices.reshape(4, 4, 2, 4, 4), ("x", "zh", "c", "y", "zl"))
    dp, seq = ("x", "zh", "c"), ("y", "zl")
    return jax.shard_map(
        local,
        mesh=fine,
        in_specs=(P(dp + seq, None), P(dp + seq, None), P(seq, dp), P(seq, dp), P(seq, dp)),
        out_specs=(P(seq, dp), P(seq, dp), P(seq, dp), P(seq, None)),
        check_vma=False,
    )
```

```python
import functools

import jax
import jax.numpy as jnp
from jax import lax
from jax.experimental import pallas as pl
from jax.experimental.pallas import tpu as pltpu
from jax.sharding import Mesh, PartitionSpec as P

D = 3072
FO = 1536
TOK = 384
F32 = jnp.float32
F16 = jnp.float16
BF16 = jnp.bfloat16


def swap(value, axis):
    return lax.ppermute(value, axis, [(0, 1), (1, 0)])


def trade(value, axes):
    return lax.all_to_all(value, axes, 0, 0, tiled=True)


def eighth(value):
    value = value * value
    value = value * value
    return value * value


def peak(ref):
    top = jnp.abs(ref[0:16, :])
    for row in range(16, TOK, 16):
        top = jnp.maximum(top, jnp.abs(ref[row:row + 16, :]))
    return jnp.max(top.astype(F32))


def arrange_kernel(core_ref, grads_ref, out_ref):
    def write(core):
        for x in range(4):
            block = grads_ref[:, x * 384:(x + 1) * 384].T
            for zh in range(4):
                to, at = (zh // 2) * 384 + x * 96 + (zh % 2) * 48, zh * 96 + core * 48
                out_ref[to:to + 48, :] = block[at:at + 48]

    @pl.when(core_ref[0] == 0)
    def _():
        write(0)

    @pl.when(core_ref[0] != 0)
    def _():
        write(1)

    out_ref[768:784, :] = jnp.full((16, TOK), peak(grads_ref), F32).astype(BF16)


def arrange(core, grads):
    vmem = pl.BlockSpec(memory_space=pltpu.VMEM)
    return pl.pallas_call(
        arrange_kernel,
        out_shape=jax.ShapeDtypeStruct((784, TOK), BF16),
        in_specs=[pl.BlockSpec(memory_space=pltpu.SMEM), vmem],
        out_specs=vmem,
        compiler_params=pltpu.CompilerParams(vmem_limit_bytes=8 << 20),
    )(core.reshape(1), grads)


def own_kernel(cols_ref, acts_ref, out_ref, peak_ref):
    peak_ref[...] = jnp.full((8, 128), peak(acts_ref), F32)
    for y in range(4):
        lanes = slice(768 * y, 768 * (y + 1))
        for half in range(2):
            rows = slice(384 * half, 384 * (half + 1))
            term = jnp.dot(cols_ref[rows, :], acts_ref[:, lanes], preferred_element_type=F32)
            out_ref[rows, lanes] = term.astype(BF16)


def own_terms(cols, acts):
    vmem = pl.BlockSpec(memory_space=pltpu.VMEM)
    return pl.pallas_call(
        own_kernel,
        out_shape=[jax.ShapeDtypeStruct((768, D), BF16), jax.ShapeDtypeStruct((8, 128), F32)],
        in_specs=[vmem, vmem],
        out_specs=[vmem, vmem],
        compiler_params=pltpu.CompilerParams(vmem_limit_bytes=14 << 20),
        cost_estimate=pl.CostEstimate(flops=2 * 768 * TOK * D, bytes_accessed=8 << 20, transcendentals=0),
    )(cols, acts)


def pair_kernel(core_ref, mine_ref, their_ref, acts_ref, own_ref, peak_ref, out_ref):
    core = core_ref[0]
    bound = peak_ref[...] * mine_ref[768:784, 0:128].astype(F32)[0:8]
    bound = TOK * (bound + peak(acts_ref) * their_ref[768:784, 0:128].astype(F32)[0:8])
    up = jnp.full((8, 128), 2.0 ** -14, F32)
    down = jnp.full((8, 128), 2.0 ** 14, F32)
    for k in range(-14, 14):
        over = bound > 2.0 ** (8 * k)
        up = jnp.where(over, up * 2.0, up)
        down = jnp.where(over, down * 0.5, down)
    scale = eighth(down[0:1, 0:1]) * 2.0 ** 15

    for half in range(2):
        rows = slice(384 * half, 384 * (half + 1))
        for y in range(4):
            lanes = slice(768 * y, 768 * (y + 1))
            term = jnp.dot(their_ref[rows, :], acts_ref[:, lanes], preferred_element_type=F32).astype(BF16)
            total = (own_ref[rows, lanes].astype(F32) + term.astype(F32)) * scale
            for x in range(4):
                u = jnp.where(core == 0, x, y)
                v = jnp.where(core == 0, y, x)
                at = pl.multiple_of(half * 384 + v * 96, 96)
                out_ref[u, pl.ds(at, 96), :] = total[x * 96:(x + 1) * 96]

    for u in range(4):
        out_ref[u, 768:776, :] = jnp.broadcast_to(up[0:1, 0:1], (8, 768))
        out_ref[u, 776:784, :] = jnp.broadcast_to(down[0:1, 0:1], (8, 768))


def pair_sums(core, mine, theirs, acts, own, own_peak):
    vmem = pl.BlockSpec(memory_space=pltpu.VMEM)
    return pl.pallas_call(
        pair_kernel,
        out_shape=jax.ShapeDtypeStruct((4, 784, 768), F32),
        in_specs=[pl.BlockSpec(memory_space=pltpu.SMEM)] + [vmem] * 5,
        out_specs=vmem,
        compiler_params=pltpu.CompilerParams(vmem_limit_bytes=24 << 20),
        cost_estimate=pl.CostEstimate(flops=2 * 768 * TOK * D, bytes_accessed=18 << 20, transcendentals=0),
    )(core.reshape(1), mine, theirs, acts, own, own_peak)


def scales(parts, rows):
    ups = [part[rows:rows + 1].astype(F32) for part in parts]
    downs = [part[rows + 8:rows + 9].astype(F32) for part in parts]
    return [eighth(up) for up in ups], functools.reduce(jnp.maximum, ups), functools.reduce(jnp.minimum, downs)


def add_parts(parts, factors, rows, top):
    return sum(part[:rows].astype(F32) * (factor * (1.0 / top)) for part, factor in zip(parts, factors))


def pack(ref, value):
    ref[0:48, :] = value[:, 0:128]
    ref[48:72, 0:64] = value[0:24, 128:192]
    ref[48:72, 64:128] = value[24:48, 128:192]


def unpack(ref, at, value):
    ref[at:at + 48, 0:128] = value[0:48]
    ref[at:at + 24, 128:192] = value[48:72, 0:64]
    ref[at + 24:at + 48, 128:192] = value[48:72, 64:128]


def z_kernel(tile_ref, up_ref, down_ref, out_ref):
    scale = eighth(down_ref[0:1, 0:1]) * 2.0 ** 11
    for zh in range(4):
        for zl in range(4):
            piece = tile_ref[zh * 48:(zh + 1) * 48, zl * 192:(zl + 1) * 192]
            pack(out_ref.at[zh * 4 + zl], piece * scale)
            out_ref[zh * 4 + zl, 72:80, :] = jnp.broadcast_to(up_ref[0:1, 0:1], (8, 128))


def z_pieces(tile, up, down):
    vmem = pl.BlockSpec(memory_space=pltpu.VMEM)
    return pl.pallas_call(
        z_kernel,
        out_shape=jax.ShapeDtypeStruct((16, 80, 128), F32),
        in_specs=[vmem, vmem, vmem],
        out_specs=vmem,
        compiler_params=pltpu.CompilerParams(vmem_limit_bytes=8 << 20),
    )(tile, up, down)


def square_kernel(grad_ref, out_ref):
    grad = grad_ref[...]
    out_ref[...] = jnp.full(out_ref.shape, jnp.sum(grad * grad), F32)


def sum_kernel(part_ref, out_ref):
    total = part_ref[0]
    for i in range(1, part_ref.shape[0]):
        total = total + part_ref[i]
    for i in range(out_ref.shape[0]):
        out_ref[i] = total


def to_send(kernel, count, value):
    vmem = pl.BlockSpec(memory_space=pltpu.VMEM)
    return pl.pallas_call(
        kernel,
        out_shape=jax.ShapeDtypeStruct((count, 1, 128), F32),
        in_specs=[vmem],
        out_specs=vmem,
        compiler_params=pltpu.CompilerParams(vmem_limit_bytes=1 << 20),
    )(value)


def update_kernel(square_ref, grad_ref, master_ref, first_ref, second_ref, *refs):
    new_master_ref, new_first_ref, new_second_ref, params_ref, tile_ref = refs
    square = square_ref[0]
    for i in range(1, 16):
        square = square + square_ref[i]
    rms = jnp.sqrt(square[:, 0:1] / (D * FO) + 1e-06)
    clip = jnp.minimum(1.0, 1.0 / rms)
    unpack(tile_ref, 0, grad_ref[...])
    clipped = clip * tile_ref[...]
    master = master_ref[...]
    new_first = 0.9 * first_ref[...] + 0.1 * clipped
    new_second = 0.95 * second_ref[...] + 0.05 * clipped * clipped
    new_master = master - 0.01 * (new_first / (jnp.sqrt(new_second) + 1e-08) + 0.1 * master)
    new_master_ref[...], new_first_ref[...], new_second_ref[...] = new_master, new_first, new_second
    for i in range(4):
        params_ref[i] = new_master.astype(BF16)


def update(square, grad, *state):
    vmem = pl.BlockSpec(memory_space=pltpu.VMEM)
    tile = jax.ShapeDtypeStruct((48, 192), F32)
    return pl.pallas_call(
        update_kernel,
        out_shape=[tile, tile, tile, jax.ShapeDtypeStruct((4, 48, 192), BF16)],
        in_specs=[vmem] * 5,
        out_specs=[vmem] * 4,
        scratch_shapes=[pltpu.VMEM((48, 192), F32)],
        compiler_params=pltpu.CompilerParams(vmem_limit_bytes=2 << 20),
    )(square, grad, *state)


def cross_trade(value, first):
    groups = []
    for core in range(2):
        for a in range(4):
            fours = [(b, core, a) if core == first else (a, core, b) for b in range(4)]
            groups.append([(x * 2 + c) * 4 + y for x, c, y in fours])
    return lax.all_to_all(value, ("x", "c", "y"), 0, 0, axis_index_groups=groups, tiled=True)


def local(acts, grads, master, first, second):
    core = lax.axis_index("c")

    their_acts = swap(acts, "c")
    their_cols = arrange(core, swap(grads, "c"))
    mine = arrange(core, grads)
    own, own_peak = own_terms(mine, acts)
    sums = pair_sums(core, mine, their_cols, their_acts, own, own_peak)
    part = cross_trade(sums.astype(F16), 0)
    parts = [part[i] for i in range(4)]
    factors, up, down = scales(parts, 768)
    total = add_parts(parts, factors, 768, 2.0 ** 15) * (eighth(down) * 2.0 ** 13)
    send = [total[:384].reshape(4, 96, 768), total[384:].reshape(4, 96, 768)]
    send += [jnp.broadcast_to(row, (4, 8, 768)) for row in (up, down)]
    part = cross_trade(jnp.concatenate([part.astype(F16) for part in send], axis=1), 1)
    parts = [part[i] for i in range(4)]
    factors, up, down = scales(parts, 192)
    tile = add_parts(parts, factors, 192, 2.0 ** 13)

    part = trade(z_pieces(tile, up, down).astype(F16), ("zh", "zl"))
    ups = part[:, 72:73, 0:1].astype(F32)
    grad = jnp.sum(part[:, :72].astype(F32) * (eighth(ups) * 2.0 ** -11), axis=0)

    square = trade(to_send(square_kernel, 32, grad), ("x", "y", "c"))
    square = trade(to_send(sum_kernel, 16, square), ("zh", "zl"))
    *outs, params = update(square, grad, master.T, first.T, second.T)
    params = trade(params, "zh")
    params = trade(jnp.broadcast_to(params, (4, 4, 48, 192)), "x").reshape(16, 48, 192)
    theirs = swap(params, "c")
    params = jnp.where(core == 0, jnp.stack([params, theirs], 1), jnp.stack([theirs, params], 1))
    return (*[out.T for out in outs], params.reshape(FO, 192).T)


def solution(mesh):
    fine = Mesh(mesh.devices.reshape(4, 4, 2, 4, 4), ("x", "zh", "c", "y", "zl"))
    dp, seq = ("x", "zh", "c"), ("y", "zl")
    return jax.shard_map(
        local,
        mesh=fine,
        in_specs=(P(dp + seq, None), P(dp + seq, None), P(seq, dp), P(seq, dp), P(seq, dp)),
        out_specs=(P(seq, dp), P(seq, dp), P(seq, dp), P(seq, None)),
        check_vma=False,
    )
```

```python
import functools

import jax
import jax.numpy as jnp
from jax import lax
from jax.experimental import pallas as pl
from jax.experimental.pallas import tpu as pltpu
from jax.sharding import Mesh, PartitionSpec as P

D = 3072
FO = 1536
TOK = 384
F32 = jnp.float32
F16 = jnp.float16
BF16 = jnp.bfloat16


def swap(value, axis):
    return lax.ppermute(value, axis, [(0, 1), (1, 0)])


def trade(value, axes):
    return lax.all_to_all(value, axes, 0, 0, tiled=True)


def eighth(value):
    value = value * value
    value = value * value
    return value * value


def peak(ref):
    top = jnp.abs(ref[0:16, :])
    for row in range(16, TOK, 16):
        top = jnp.maximum(top, jnp.abs(ref[row:row + 16, :]))
    return jnp.max(top.astype(F32))


def arrange_kernel(core_ref, grads_ref, out_ref):
    def write(core):
        for x in range(4):
            block = grads_ref[:, x * 384:(x + 1) * 384].T
            for zh in range(4):
                to, at = (zh // 2) * 384 + x * 96 + (zh % 2) * 48, zh * 96 + core * 48
                out_ref[to:to + 48, :] = block[at:at + 48]

    @pl.when(core_ref[0] == 0)
    def _():
        write(0)

    @pl.when(core_ref[0] != 0)
    def _():
        write(1)

    out_ref[768:784, :] = jnp.full((16, TOK), peak(grads_ref), F32).astype(BF16)


def arrange(core, grads):
    vmem = pl.BlockSpec(memory_space=pltpu.VMEM)
    return pl.pallas_call(
        arrange_kernel,
        out_shape=jax.ShapeDtypeStruct((784, TOK), BF16),
        in_specs=[pl.BlockSpec(memory_space=pltpu.SMEM), vmem],
        out_specs=vmem,
        compiler_params=pltpu.CompilerParams(vmem_limit_bytes=8 << 20),
    )(core.reshape(1), grads)


def own_kernel(cols_ref, acts_ref, out_ref, peak_ref):
    peak_ref[...] = jnp.full((8, 128), peak(acts_ref), F32)
    for y in range(4):
        lanes = slice(768 * y, 768 * (y + 1))
        for half in range(2):
            rows = slice(384 * half, 384 * (half + 1))
            term = jnp.dot(cols_ref[rows, :], acts_ref[:, lanes], preferred_element_type=F32)
            out_ref[rows, lanes] = term.astype(BF16)


def own_terms(cols, acts):
    vmem = pl.BlockSpec(memory_space=pltpu.VMEM)
    return pl.pallas_call(
        own_kernel,
        out_shape=[jax.ShapeDtypeStruct((768, D), BF16), jax.ShapeDtypeStruct((8, 128), F32)],
        in_specs=[vmem, vmem],
        out_specs=[vmem, vmem],
        compiler_params=pltpu.CompilerParams(vmem_limit_bytes=14 << 20),
        cost_estimate=pl.CostEstimate(flops=2 * 768 * TOK * D, bytes_accessed=8 << 20, transcendentals=0),
    )(cols, acts)


def pair_kernel(core_ref, mine_ref, their_ref, acts_ref, own_ref, peak_ref, out_ref):
    core = core_ref[0]
    bound = peak_ref[...] * mine_ref[768:784, 0:128].astype(F32)[0:8]
    bound = TOK * (bound + peak(acts_ref) * their_ref[768:784, 0:128].astype(F32)[0:8])
    up = jnp.full((8, 128), 2.0 ** -14, F32)
    down = jnp.full((8, 128), 2.0 ** 14, F32)
    for k in range(-14, 14):
        over = bound > 2.0 ** (8 * k)
        up = jnp.where(over, up * 2.0, up)
        down = jnp.where(over, down * 0.5, down)
    scale = eighth(down[0:1, 0:1]) * 2.0 ** 15

    for half in range(2):
        rows = slice(384 * half, 384 * (half + 1))
        for y in range(4):
            lanes = slice(768 * y, 768 * (y + 1))
            term = jnp.dot(their_ref[rows, :], acts_ref[:, lanes], preferred_element_type=F32).astype(BF16)
            total = (own_ref[rows, lanes].astype(F32) + term.astype(F32)) * scale
            for x in range(4):
                u = jnp.where(core == 0, x, y)
                v = jnp.where(core == 0, y, x)
                at = pl.multiple_of(half * 384 + v * 96, 96)
                out_ref[u, pl.ds(at, 96), :] = total[x * 96:(x + 1) * 96]

    for u in range(4):
        out_ref[u, 768:776, :] = jnp.broadcast_to(up[0:1, 0:1], (8, 768))


def pair_sums(core, mine, theirs, acts, own, own_peak):
    vmem = pl.BlockSpec(memory_space=pltpu.VMEM)
    return pl.pallas_call(
        pair_kernel,
        out_shape=jax.ShapeDtypeStruct((4, 776, 768), F32),
        in_specs=[pl.BlockSpec(memory_space=pltpu.SMEM)] + [vmem] * 5,
        out_specs=vmem,
        compiler_params=pltpu.CompilerParams(vmem_limit_bytes=24 << 20),
        cost_estimate=pl.CostEstimate(flops=2 * 768 * TOK * D, bytes_accessed=18 << 20, transcendentals=0),
    )(core.reshape(1), mine, theirs, acts, own, own_peak)


def scales(parts, rows):
    ups = [part[rows:rows + 1].astype(F32) for part in parts]
    up = functools.reduce(jnp.maximum, ups)
    return [eighth(one) for one in ups], up, 1.0 / up


def add_parts(parts, factors, rows, top):
    return sum(part[:rows].astype(F32) * (factor * (1.0 / top)) for part, factor in zip(parts, factors))


def pack(ref, value):
    ref[0:48, :] = value[:, 0:128]
    ref[48:72, 0:64] = value[0:24, 128:192]
    ref[48:72, 64:128] = value[24:48, 128:192]


def unpack(ref, at, value):
    ref[at:at + 48, 0:128] = value[0:48]
    ref[at:at + 24, 128:192] = value[48:72, 0:64]
    ref[at + 24:at + 48, 128:192] = value[48:72, 64:128]


def z_kernel(tile_ref, up_ref, down_ref, out_ref):
    scale = eighth(down_ref[0:1, 0:1]) * 2.0 ** 11
    for zh in range(4):
        for zl in range(4):
            piece = tile_ref[zh * 48:(zh + 1) * 48, zl * 192:(zl + 1) * 192]
            pack(out_ref.at[zh * 4 + zl], piece * scale)
            out_ref[zh * 4 + zl, 72:80, :] = jnp.broadcast_to(up_ref[0:1, 0:1], (8, 128))


def z_pieces(tile, up, down):
    vmem = pl.BlockSpec(memory_space=pltpu.VMEM)
    return pl.pallas_call(
        z_kernel,
        out_shape=jax.ShapeDtypeStruct((16, 80, 128), F32),
        in_specs=[vmem, vmem, vmem],
        out_specs=vmem,
        compiler_params=pltpu.CompilerParams(vmem_limit_bytes=8 << 20),
    )(tile, up, down)


def square_kernel(grad_ref, out_ref):
    grad = grad_ref[...]
    out_ref[...] = jnp.full(out_ref.shape, jnp.sum(grad * grad), F32)


def sum_kernel(part_ref, out_ref):
    total = part_ref[0]
    for i in range(1, part_ref.shape[0]):
        total = total + part_ref[i]
    for i in range(out_ref.shape[0]):
        out_ref[i] = total


def to_send(kernel, count, value):
    vmem = pl.BlockSpec(memory_space=pltpu.VMEM)
    return pl.pallas_call(
        kernel,
        out_shape=jax.ShapeDtypeStruct((count, 1, 128), F32),
        in_specs=[vmem],
        out_specs=vmem,
        compiler_params=pltpu.CompilerParams(vmem_limit_bytes=1 << 20),
    )(value)


def update_kernel(square_ref, grad_ref, master_ref, first_ref, second_ref, *refs):
    new_master_ref, new_first_ref, new_second_ref, params_ref, tile_ref = refs
    square = square_ref[0]
    for i in range(1, 16):
        square = square + square_ref[i]
    rms = jnp.sqrt(square[:, 0:1] / (D * FO) + 1e-06)
    clip = jnp.minimum(1.0, 1.0 / rms)
    unpack(tile_ref, 0, grad_ref[...])
    clipped = clip * tile_ref[...]
    master = master_ref[...]
    new_first = 0.9 * first_ref[...] + 0.1 * clipped
    new_second = 0.95 * second_ref[...] + 0.05 * clipped * clipped
    new_master = master - 0.01 * (new_first / (jnp.sqrt(new_second) + 1e-08) + 0.1 * master)
    new_master_ref[...], new_first_ref[...], new_second_ref[...] = new_master, new_first, new_second
    for i in range(4):
        params_ref[i] = new_master.astype(BF16)


def update(square, grad, *state):
    vmem = pl.BlockSpec(memory_space=pltpu.VMEM)
    tile = jax.ShapeDtypeStruct((48, 192), F32)
    return pl.pallas_call(
        update_kernel,
        out_shape=[tile, tile, tile, jax.ShapeDtypeStruct((4, 48, 192), BF16)],
        in_specs=[vmem] * 5,
        out_specs=[vmem] * 4,
        scratch_shapes=[pltpu.VMEM((48, 192), F32)],
        compiler_params=pltpu.CompilerParams(vmem_limit_bytes=2 << 20),
    )(square, grad, *state)


def cross_trade(value, first):
    groups = []
    for core in range(2):
        for a in range(4):
            fours = [(b, core, a) if core == first else (a, core, b) for b in range(4)]
            groups.append([(x * 2 + c) * 4 + y for x, c, y in fours])
    return lax.all_to_all(value, ("x", "c", "y"), 0, 0, axis_index_groups=groups, tiled=True)


def local(acts, grads, master, first, second):
    core = lax.axis_index("c")

    their_acts = swap(acts, "c")
    their_cols = arrange(core, swap(grads, "c"))
    mine = arrange(core, grads)
    own, own_peak = own_terms(mine, acts)
    sums = pair_sums(core, mine, their_cols, their_acts, own, own_peak)
    part = cross_trade(sums.astype(F16), 0)
    parts = [part[i] for i in range(4)]
    factors, up, down = scales(parts, 768)
    total = add_parts(parts, factors, 768, 2.0 ** 15) * (eighth(down) * 2.0 ** 13)
    send = [total[:384].reshape(4, 96, 768), total[384:].reshape(4, 96, 768)]
    send.append(jnp.broadcast_to(up, (4, 8, 768)))
    part = cross_trade(jnp.concatenate([part.astype(F16) for part in send], axis=1), 1)
    parts = [part[i] for i in range(4)]
    factors, up, down = scales(parts, 192)
    tile = add_parts(parts, factors, 192, 2.0 ** 13)

    part = trade(z_pieces(tile, up, down).astype(F16), ("zh", "zl"))
    ups = part[:, 72:73, 0:1].astype(F32)
    grad = jnp.sum(part[:, :72].astype(F32) * (eighth(ups) * 2.0 ** -11), axis=0)

    square = trade(to_send(square_kernel, 32, grad), ("x", "y", "c"))
    square = trade(to_send(sum_kernel, 16, square), ("zh", "zl"))
    *outs, params = update(square, grad, master.T, first.T, second.T)
    params = trade(params, "zh")
    params = trade(jnp.broadcast_to(params, (4, 4, 48, 192)), "x").reshape(16, 48, 192)
    theirs = swap(params, "c")
    params = jnp.where(core == 0, jnp.stack([params, theirs], 1), jnp.stack([theirs, params], 1))
    return (*[out.T for out in outs], params.reshape(FO, 192).T)


def solution(mesh):
    fine = Mesh(mesh.devices.reshape(4, 4, 2, 4, 4), ("x", "zh", "c", "y", "zl"))
    dp, seq = ("x", "zh", "c"), ("y", "zl")
    return jax.shard_map(
        local,
        mesh=fine,
        in_specs=(P(dp + seq, None), P(dp + seq, None), P(seq, dp), P(seq, dp), P(seq, dp)),
        out_specs=(P(seq, dp), P(seq, dp), P(seq, dp), P(seq, None)),
        check_vma=False,
    )
```

```python
import functools

import jax
import jax.numpy as jnp
from jax import lax
from jax.experimental import pallas as pl
from jax.experimental.pallas import tpu as pltpu
from jax.sharding import Mesh, PartitionSpec as P

D = 3072
FO = 1536
TOK = 384
F32 = jnp.float32
F16 = jnp.float16
BF16 = jnp.bfloat16


def swap(value, axis):
    return lax.ppermute(value, axis, [(0, 1), (1, 0)])


def trade(value, axes):
    return lax.all_to_all(value, axes, 0, 0, tiled=True)


def eighth(value):
    value = value * value
    value = value * value
    return value * value


def peak(ref):
    top = jnp.abs(ref[0:16, :])
    for row in range(16, TOK, 16):
        top = jnp.maximum(top, jnp.abs(ref[row:row + 16, :]))
    return jnp.max(top.astype(F32))


def arrange_kernel(core_ref, grads_ref, out_ref):
    def write(core):
        for x in range(4):
            block = grads_ref[:, x * 384:(x + 1) * 384].T
            for zh in range(4):
                to, at = (zh // 2) * 384 + x * 96 + (zh % 2) * 48, zh * 96 + core * 48
                out_ref[to:to + 48, :] = block[at:at + 48]

    @pl.when(core_ref[0] == 0)
    def _():
        write(0)

    @pl.when(core_ref[0] != 0)
    def _():
        write(1)

    out_ref[768:784, :] = jnp.full((16, TOK), peak(grads_ref), F32).astype(BF16)


def arrange(core, grads):
    vmem = pl.BlockSpec(memory_space=pltpu.VMEM)
    return pl.pallas_call(
        arrange_kernel,
        out_shape=jax.ShapeDtypeStruct((784, TOK), BF16),
        in_specs=[pl.BlockSpec(memory_space=pltpu.SMEM), vmem],
        out_specs=vmem,
        compiler_params=pltpu.CompilerParams(vmem_limit_bytes=8 << 20),
    )(core.reshape(1), grads)


def own_kernel(cols_ref, acts_ref, out_ref, peak_ref):
    peak_ref[...] = jnp.full((8, 128), peak(acts_ref), F32)
    for y in range(4):
        lanes = slice(768 * y, 768 * (y + 1))
        term = jnp.dot(cols_ref[0:768, :], acts_ref[:, lanes], preferred_element_type=F32)
        out_ref[:, lanes] = term.astype(BF16)


def own_terms(cols, acts):
    vmem = pl.BlockSpec(memory_space=pltpu.VMEM)
    return pl.pallas_call(
        own_kernel,
        out_shape=[jax.ShapeDtypeStruct((768, D), BF16), jax.ShapeDtypeStruct((8, 128), F32)],
        in_specs=[vmem, vmem],
        out_specs=[vmem, vmem],
        compiler_params=pltpu.CompilerParams(vmem_limit_bytes=14 << 20),
        cost_estimate=pl.CostEstimate(flops=2 * 768 * TOK * D, bytes_accessed=8 << 20, transcendentals=0),
    )(cols, acts)


def pair_kernel(core_ref, mine_ref, their_ref, acts_ref, own_ref, peak_ref, out_ref):
    core = core_ref[0]
    bound = peak_ref[...] * mine_ref[768:784, 0:128].astype(F32)[0:8]
    bound = TOK * (bound + peak(acts_ref) * their_ref[768:784, 0:128].astype(F32)[0:8])
    up = jnp.full((8, 128), 2.0 ** -14, F32)
    down = jnp.full((8, 128), 2.0 ** 14, F32)
    for k in range(-14, 14):
        over = bound > 2.0 ** (8 * k)
        up = jnp.where(over, up * 2.0, up)
        down = jnp.where(over, down * 0.5, down)
    scale = eighth(down[0:1, 0:1]) * 2.0 ** 15

    for half in range(2):
        rows = slice(384 * half, 384 * (half + 1))
        for y in range(4):
            lanes = slice(768 * y, 768 * (y + 1))
            term = jnp.dot(their_ref[rows, :], acts_ref[:, lanes], preferred_element_type=F32).astype(BF16)
            total = (own_ref[rows, lanes].astype(F32) + term.astype(F32)) * scale
            for x in range(4):
                u = jnp.where(core == 0, x, y)
                v = jnp.where(core == 0, y, x)
                at = pl.multiple_of(half * 384 + v * 96, 96)
                out_ref[u, pl.ds(at, 96), :] = total[x * 96:(x + 1) * 96]

    for u in range(4):
        out_ref[u, 768:776, :] = jnp.broadcast_to(up[0:1, 0:1], (8, 768))


def pair_sums(core, mine, theirs, acts, own, own_peak):
    vmem = pl.BlockSpec(memory_space=pltpu.VMEM)
    return pl.pallas_call(
        pair_kernel,
        out_shape=jax.ShapeDtypeStruct((4, 776, 768), F32),
        in_specs=[pl.BlockSpec(memory_space=pltpu.SMEM)] + [vmem] * 5,
        out_specs=vmem,
        compiler_params=pltpu.CompilerParams(vmem_limit_bytes=24 << 20),
        cost_estimate=pl.CostEstimate(flops=2 * 768 * TOK * D, bytes_accessed=18 << 20, transcendentals=0),
    )(core.reshape(1), mine, theirs, acts, own, own_peak)


def scales(parts, rows):
    ups = [part[rows:rows + 1].astype(F32) for part in parts]
    up = functools.reduce(jnp.maximum, ups)
    return [eighth(one) for one in ups], up, 1.0 / up


def add_parts(parts, factors, rows, top):
    return sum(part[:rows].astype(F32) * (factor * (1.0 / top)) for part, factor in zip(parts, factors))


def pack(ref, value):
    ref[0:48, :] = value[:, 0:128]
    ref[48:72, 0:64] = value[0:24, 128:192]
    ref[48:72, 64:128] = value[24:48, 128:192]


def unpack(ref, at, value):
    ref[at:at + 48, 0:128] = value[0:48]
    ref[at:at + 24, 128:192] = value[48:72, 0:64]
    ref[at + 24:at + 48, 128:192] = value[48:72, 64:128]


def z_kernel(tile_ref, up_ref, down_ref, out_ref):
    scale = eighth(down_ref[0:1, 0:1]) * 2.0 ** 11
    for zh in range(4):
        for zl in range(4):
            piece = tile_ref[zh * 48:(zh + 1) * 48, zl * 192:(zl + 1) * 192]
            pack(out_ref.at[zh * 4 + zl], piece * scale)
            out_ref[zh * 4 + zl, 72:80, :] = jnp.broadcast_to(up_ref[0:1, 0:1], (8, 128))


def z_pieces(tile, up, down):
    vmem = pl.BlockSpec(memory_space=pltpu.VMEM)
    return pl.pallas_call(
        z_kernel,
        out_shape=jax.ShapeDtypeStruct((16, 80, 128), F32),
        in_specs=[vmem, vmem, vmem],
        out_specs=vmem,
        compiler_params=pltpu.CompilerParams(vmem_limit_bytes=8 << 20),
    )(tile, up, down)


def square_kernel(grad_ref, out_ref):
    grad = grad_ref[...]
    out_ref[...] = jnp.full(out_ref.shape, jnp.sum(grad * grad), F32)


def sum_kernel(part_ref, out_ref):
    total = part_ref[0]
    for i in range(1, part_ref.shape[0]):
        total = total + part_ref[i]
    for i in range(out_ref.shape[0]):
        out_ref[i] = total


def to_send(kernel, count, value):
    vmem = pl.BlockSpec(memory_space=pltpu.VMEM)
    return pl.pallas_call(
        kernel,
        out_shape=jax.ShapeDtypeStruct((count, 1, 128), F32),
        in_specs=[vmem],
        out_specs=vmem,
        compiler_params=pltpu.CompilerParams(vmem_limit_bytes=1 << 20),
    )(value)


def update_kernel(square_ref, grad_ref, master_ref, first_ref, second_ref, *refs):
    new_master_ref, new_first_ref, new_second_ref, params_ref, tile_ref = refs
    square = square_ref[0]
    for i in range(1, 16):
        square = square + square_ref[i]
    rms = jnp.sqrt(square[:, 0:1] / (D * FO) + 1e-06)
    clip = jnp.minimum(1.0, 1.0 / rms)
    unpack(tile_ref, 0, grad_ref[...])
    clipped = clip * tile_ref[...]
    master = master_ref[...]
    new_first = 0.9 * first_ref[...] + 0.1 * clipped
    new_second = 0.95 * second_ref[...] + 0.05 * clipped * clipped
    new_master = master - 0.01 * (new_first / (jnp.sqrt(new_second) + 1e-08) + 0.1 * master)
    new_master_ref[...], new_first_ref[...], new_second_ref[...] = new_master, new_first, new_second
    for i in range(4):
        params_ref[i] = new_master.astype(BF16)


def update(square, grad, *state):
    vmem = pl.BlockSpec(memory_space=pltpu.VMEM)
    tile = jax.ShapeDtypeStruct((48, 192), F32)
    return pl.pallas_call(
        update_kernel,
        out_shape=[tile, tile, tile, jax.ShapeDtypeStruct((4, 48, 192), BF16)],
        in_specs=[vmem] * 5,
        out_specs=[vmem] * 4,
        scratch_shapes=[pltpu.VMEM((48, 192), F32)],
        compiler_params=pltpu.CompilerParams(vmem_limit_bytes=2 << 20),
    )(square, grad, *state)


def cross_trade(value, first):
    groups = []
    for core in range(2):
        for a in range(4):
            fours = [(b, core, a) if core == first else (a, core, b) for b in range(4)]
            groups.append([(x * 2 + c) * 4 + y for x, c, y in fours])
    return lax.all_to_all(value, ("x", "c", "y"), 0, 0, axis_index_groups=groups, tiled=True)


def local(acts, grads, master, first, second):
    core = lax.axis_index("c")

    their_acts = swap(acts, "c")
    their_cols = arrange(core, swap(grads, "c"))
    mine = arrange(core, grads)
    own, own_peak = own_terms(mine, acts)
    sums = pair_sums(core, mine, their_cols, their_acts, own, own_peak)
    part = cross_trade(sums.astype(F16), 0)
    parts = [part[i] for i in range(4)]
    factors, up, down = scales(parts, 768)
    total = add_parts(parts, factors, 768, 2.0 ** 15) * (eighth(down) * 2.0 ** 13)
    send = [total[:384].reshape(4, 96, 768), total[384:].reshape(4, 96, 768)]
    send.append(jnp.broadcast_to(up, (4, 8, 768)))
    part = cross_trade(jnp.concatenate([part.astype(F16) for part in send], axis=1), 1)
    parts = [part[i] for i in range(4)]
    factors, up, down = scales(parts, 192)
    tile = add_parts(parts, factors, 192, 2.0 ** 13)

    part = trade(z_pieces(tile, up, down).astype(F16), ("zh", "zl"))
    ups = part[:, 72:73, 0:1].astype(F32)
    grad = jnp.sum(part[:, :72].astype(F32) * (eighth(ups) * 2.0 ** -11), axis=0)

    square = trade(to_send(square_kernel, 32, grad), ("x", "y", "c"))
    square = trade(to_send(sum_kernel, 16, square), ("zh", "zl"))
    *outs, params = update(square, grad, master.T, first.T, second.T)
    params = trade(params, "zh")
    params = trade(jnp.broadcast_to(params, (4, 4, 48, 192)), "x").reshape(16, 48, 192)
    theirs = swap(params, "c")
    params = jnp.where(core == 0, jnp.stack([params, theirs], 1), jnp.stack([theirs, params], 1))
    return (*[out.T for out in outs], params.reshape(FO, 192).T)


def solution(mesh):
    fine = Mesh(mesh.devices.reshape(4, 4, 2, 4, 4), ("x", "zh", "c", "y", "zl"))
    dp, seq = ("x", "zh", "c"), ("y", "zl")
    return jax.shard_map(
        local,
        mesh=fine,
        in_specs=(P(dp + seq, None), P(dp + seq, None), P(seq, dp), P(seq, dp), P(seq, dp)),
        out_specs=(P(seq, dp), P(seq, dp), P(seq, dp), P(seq, None)),
        check_vma=False,
    )
```
